32 devices in a mesh: member: 8 (over z, core), state: 4 (over y, x).
Axes of the slice: x: 2, y: 2, z: 4, core: 2. Of those that a mesh axis runs over, the one named last changes fastest.
Arguments:
- prior_analyses: float32 [64, 256, 1024], P('member', 'state'), may hold values from -6 to 6
- smoothing_number: float32 [256, 1024], P('state'), may hold values from 0.08 to 0.24
- observations: float32 [3072], replicated, may hold values from -6 to 6
- obs_variance: float32 [3072], replicated, may hold values from 0.25 to 2
- obs_row: int32 [3072], replicated, may hold values from 0 to 255
- obs_col: int32 [3072], replicated, may hold values from 0 to 1023
- obs_radius: int32 [3072], replicated, may hold values from 32 to 127
- block_order: int32 [3072], replicated, may hold values from 0 to 3071, each once
Outputs:
- analysis: float32 [64, 256, 1024], P('member', 'state')
The draws below stay inside these ranges and needn't reach their ends.
Inputs may be any that keep to these rules, and one draw needn't show every extreme that they name: `block_order`: every observation index appears exactly once.
All inputs are finite; a program needn't handle non-finite values.
Results may differ from the reference program's by a relative error of at most 0.0035.
Values sent between devices are 32-bit elements; how exact they have to be, the bound alone decides.
A program may use at most 64 MiB of HBM per device.

```python
import math
import jax
import jax.numpy as jnp
from jax import lax

M = 64
NY = 1024
R = 64
BLK = 512
NBLK = 6
NX = 256
NOBS = 3072
RAD_LO = 32
RAD_HI = 128
N_STATE = 4


def touch_ends(drawn, key, low, top_value):
    index_at = [jax.random.randint(jax.random.fold_in(key, axis), (), 0, length) for axis, length in enumerate(drawn.shape)]
    longest = drawn.shape.index(max(drawn.shape))
    neighbour = index_at[:longest] + [(index_at[longest] + 1) % drawn.shape[longest]] + index_at[longest + 1:]
    return drawn.at[tuple(index_at)].set(low).at[tuple(neighbour)].set(top_value)


def block_scale(key, shape, split, least, top_value):
    level = 1.0
    for axis_at, shards_of in split:
        heights = jax.random.uniform(jax.random.fold_in(jax.random.fold_in(key, 6), axis_at), (shards_of,), jnp.float32, least / len(split), top_value / len(split))
        level = level * jnp.repeat(jnp.exp(heights), shape[axis_at] // shards_of).reshape((-1,) + (1,) * (len(shape) - 1 - axis_at))
    return level


def bell_draw(key, shape, scale, limit, cuts=(), kind=jnp.bfloat16):
    values = jax.random.normal(key, shape, jnp.float32) * scale
    if len(cuts) > 0:
        values = block_scale(key, shape, cuts, -0.22, 0.18) * values
    return jnp.clip(values, min=-limit, max=limit).astype(kind)


def setup_inputs(seed: int = 0) -> dict:
    streams_of = jax.random.split(jax.random.key(seed), 9)
    return {
        "prior_analyses": bell_draw(streams_of[0], (M, NX, NY), 1.0, 6.0, ((0, 8), (1, 4)), jnp.float32),
        "smoothing_number": jnp.clip(0.08 + 0.16 * jax.random.uniform(streams_of[1], (NX, NY), jnp.float32) ** block_scale(streams_of[1], (NX, NY), ((0, 4),), -0.2, 0.2), 0.08, 0.24),
        "observations": bell_draw(streams_of[2], (NOBS,), 1.5, 6.0, (), jnp.float32),
        "obs_variance": jnp.clip(jnp.exp(jax.random.uniform(streams_of[3], (NOBS,), jnp.float32, math.log(0.25), math.log(2.0))), 0.25, 2.0),
        "obs_row": touch_ends(jax.random.randint(streams_of[4], (NOBS,), 0, NX), jax.random.fold_in(streams_of[4], 1), 0, NX - 1).astype(jnp.int32),
        "obs_col": touch_ends(jax.random.randint(streams_of[5], (NOBS,), 0, NY), jax.random.fold_in(streams_of[5], 1), 0, NY - 1).astype(jnp.int32),
        "obs_radius": touch_ends(jax.random.randint(streams_of[6], (NOBS,), RAD_LO, RAD_HI), jax.random.fold_in(streams_of[6], 1), RAD_LO, RAD_HI - 1).astype(jnp.int32),
        "block_order": jax.random.permutation(streams_of[7], NOBS).astype(jnp.int32),
    }


spread_eps = 1e-06

def advance(field_now, spreading_coefficients):
    padded = jnp.pad(field_now, ((0, 0), (1, 1), (1, 1)))
    beside_all = padded[:, 2:, 1:-1] + padded[:, :-2, 1:-1] + padded[:, 1:-1, 2:] + padded[:, 1:-1, :-2]
    return field_now + spreading_coefficients * (beside_all - 4.0 * field_now)

def increments(prior_values, value_array, variances):
    realization_vectors = prior_values.shape[0]
    prior_mean = lax.optimization_barrier(jnp.mean(prior_values, axis=0))
    anomaly = prior_values - prior_mean
    spread = lax.optimization_barrier(jnp.sum(anomaly * anomaly, axis=0)) / (realization_vectors - 1) + spread_eps
    post_var = spread * variances / (spread + variances)
    posterior_average = post_var * (prior_mean / spread + value_array / variances)
    shrink = jnp.sqrt(variances / (variances + spread)) - 1.0
    increment = (posterior_average - prior_mean + shrink * anomaly).astype(jnp.bfloat16)
    return (anomaly.astype(jnp.bfloat16), increment, 1.0 / spread)

def taper_weight(cell_row, cell_col, obs_rows, obs_cols, radius):
    row_gap = cell_row[None, :] - obs_rows[:, None]
    col_gap = cell_col[None, :] - obs_cols[:, None]
    distance = (row_gap * row_gap + col_gap * col_gap).astype(jnp.float32)
    reach = radius.astype(jnp.float32)
    closeness = jnp.maximum(1.0 - distance / (reach * reach)[:, None], 0.0)
    return closeness * closeness

def reference(prior_analyses, smoothing_number, observations, obs_variance, obs_row, obs_col, obs_radius, block_order):
    state_now = prior_analyses
    for step_index in range(2):
        state_now = advance(state_now, smoothing_number)
    realization_vectors = state_now.shape[0]
    flat = state_now.reshape(realization_vectors, NX * NY)
    for block_index in range(NBLK):
        chosen = block_order[block_index * BLK:(block_index + 1) * BLK]
        block_rows = jnp.take(obs_row, chosen)
        block_cols = jnp.take(obs_col, chosen)
        block_radius = jnp.take(obs_radius, chosen)
        prior_values = jnp.take(flat, (block_rows * NY + block_cols).astype(jnp.int32), axis=1)
        anomaly, increment, inverse = increments(prior_values, jnp.take(observations, chosen), jnp.take(obs_variance, chosen))
        pieces = flat.reshape(realization_vectors, N_STATE, R * NY).transpose(1, 0, 2)

        def piece_update(passed_along):
            piece, piece_index = passed_along
            position = jnp.arange(R * NY, dtype=jnp.int32)
            cell_row = piece_index * R + position // NY
            cell_col = position % NY
            cell_mean = lax.optimization_barrier(jnp.mean(piece, axis=0))
            cell_anomaly = (piece - cell_mean).astype(jnp.bfloat16)
            covariance = jnp.dot(anomaly.T.astype(jnp.float32), cell_anomaly.astype(jnp.float32), precision=lax.Precision.HIGHEST) / (realization_vectors - 1)
            weight = taper_weight(cell_row, cell_col, block_rows, block_cols, block_radius)
            gain_tile = (weight * covariance * inverse[:, None]).astype(jnp.bfloat16)
            return piece + jnp.dot(increment.astype(jnp.float32), gain_tile.astype(jnp.float32), precision=lax.Precision.HIGHEST)
        updated_state = lax.map(piece_update, (pieces, jnp.arange(N_STATE, dtype=jnp.int32)))
        flat = updated_state.transpose(1, 0, 2).reshape(realization_vectors, NX * NY)
    return flat.reshape(realization_vectors, NX, NY)
```

```python
import functools

import jax
import jax.numpy as jnp
from jax import lax
from jax.experimental import pallas as pl
from jax.experimental.pallas import tpu as pltpu
from jax.sharding import PartitionSpec as P

BLK = 512
NBLK = 6
LANES = 128
TILE = 256
EPS = 1e-06
MESH = pl.DeviceIdType.MESH
VMEM = pl.BlockSpec(memory_space=pltpu.VMEM)
SMEM = pl.BlockSpec(memory_space=pltpu.SMEM)


def forecast(u, coef):
    peers = lax.axis_size("state")
    up = [(i, i + 1) for i in range(peers - 1)]
    down = [(j, i) for i, j in up]
    rows = u.shape[1]
    both = jnp.concatenate([u, coef[None]], axis=0)
    before = lax.ppermute(both[:, rows - 2 :], "state", up)
    after = lax.ppermute(both[:, :2], "state", down)
    full = jnp.concatenate([before, both, after], axis=1)
    current, field = full[:-1], full[-1]
    for _ in range(2):
        center = current[:, 1:-1]
        field = field[1:-1]
        vertical = current[:, 2:] + current[:, :-2]
        sideways = jnp.pad(center[:, :, 1:], ((0, 0), (0, 0), (0, 1))) + jnp.pad(
            center[:, :, :-1], ((0, 0), (0, 0), (1, 0))
        )
        current = center + field * (vertical + sideways - 4.0 * center)
    return current


def pick_kernel(base_ref, row_ref, col_ref, field_ref, out_ref):
    rows, members, _ = field_ref.shape
    base = base_ref[0]
    lane = lax.broadcasted_iota(jnp.int32, (members, LANES), 1)

    def chunk(j, _):
        def step(t, acc):
            for i in range(8):
                at = t * 8 + i
                k = j * LANES + at
                local = row_ref[k] - base
                col = col_ref[k]
                inside = (local >= 0) & (local < rows)
                local = jnp.clip(local, 0, rows - 1)
                start = pl.multiple_of((col // LANES) * LANES, LANES)
                part = field_ref[local, :, pl.ds(start, LANES)]
                turned = pltpu.roll(part, (at - col + 8 * LANES * 64) % LANES, 1)
                target = jnp.where(inside, at, -1)
                acc = jnp.where(lane == target, turned, acc)
            return acc

        acc = lax.fori_loop(0, LANES // 8, step, jnp.zeros((members, LANES), jnp.float32))
        out_ref[:, pl.ds(pl.multiple_of(j * LANES, LANES), LANES)] = acc
        return 0

    lax.fori_loop(0, out_ref.shape[1] // LANES, chunk, 0)


def share_kernel(n_member, n_state, part_ref, out_ref, slots, send_s, recv_s, send_m, recv_m):
    mi = lax.axis_index("member")
    si = lax.axis_index("state")
    barrier = pltpu.get_barrier_semaphore()
    for d in range(1, n_state):
        peer = lax.rem(si + d, n_state)
        pl.semaphore_signal(barrier, inc=1, device_id=(mi, peer), device_id_type=MESH)
    for d in range(1, n_member):
        peer = lax.rem(mi + d, n_member)
        pl.semaphore_signal(barrier, inc=1, device_id=(peer, si), device_id_type=MESH)
    pl.semaphore_wait(barrier, n_state + n_member - 2)
    first = []
    for d in range(1, n_state):
        peer = lax.rem(si + d, n_state)
        copy = pltpu.make_async_remote_copy(
            src_ref=part_ref,
            dst_ref=slots.at[d - 1],
            send_sem=send_s.at[d - 1],
            recv_sem=recv_s.at[d - 1],
            device_id=(mi, peer),
            device_id_type=MESH,
        )
        copy.start()
        first.append(copy)
    total = part_ref[...]
    for d in range(1, n_state):
        first[d - 1].wait()
        total = total + slots[d - 1]
    out_ref[mi] = total
    second = []
    for d in range(1, n_member):
        peer = lax.rem(mi + d, n_member)
        copy = pltpu.make_async_remote_copy(
            src_ref=out_ref.at[mi],
            dst_ref=out_ref.at[mi],
            send_sem=send_m.at[d - 1],
            recv_sem=recv_m.at[d - 1],
            device_id=(peer, si),
            device_id_type=MESH,
        )
        copy.start()
        second.append(copy)
    for copy in second:
        copy.wait()


def assimilate_kernel(
    base_ref, x_ref, y0_ref, pcol_ref, prow_ref, out_ref, y_ref, near_ref, across_ref, ybt_ref, dy_ref, q_ref
):
    rows, members, cols = x_ref.shape
    base = base_ref[0].astype(jnp.float32)
    out_ref[...] = x_ref[...]
    y_ref[...] = y0_ref[...]
    groups = TILE // LANES

    def anomalies(values):
        return (values - jnp.mean(values, axis=0, keepdims=True)).astype(jnp.bfloat16)

    def block(b, _):
        own = pl.ds(pl.multiple_of(b * BLK, BLK), BLK)
        values = y_ref[:, own]
        mean = jnp.mean(values, axis=0, keepdims=True)
        anomaly = values - mean
        spread = jnp.sum(anomaly * anomaly, axis=0, keepdims=True) / (members - 1) + EPS
        observed = prow_ref[3:4, own]
        variance = prow_ref[4:5, own]
        post = spread * variance / (spread + variance)
        center = post * (mean / spread + observed / variance)
        shrink = jnp.sqrt(variance / (variance + spread)) - 1.0
        dy_ref[...] = (center - mean + shrink * anomaly).astype(jnp.bfloat16)
        turned = anomaly.T
        ybt_ref[...] = turned.astype(jnp.bfloat16)
        spread_c = jnp.sum(turned * turned, axis=1, keepdims=True) / (members - 1) + EPS
        q = jnp.sqrt(1.0 / (spread_c * (members - 1)))
        obs_r = pcol_ref[own, 0:1]
        obs_c = pcol_ref[own, 1:2]
        reach = pcol_ref[own, 2:3]
        inv = q / (reach * reach)
        q_ref[:, 0:1] = q
        q_ref[:, 1:2] = inv
        for r in range(rows):
            gap = base + float(r) - obs_r
            near_ref[r] = jnp.broadcast_to(q - gap * gap * inv, (BLK, LANES))

        def column(t, _):
            at = pl.ds(pl.multiple_of(t * TILE, TILE), TILE)
            place = (lax.broadcasted_iota(jnp.int32, (1, TILE), 1) + t * TILE).astype(jnp.float32)
            gap = place - obs_c
            across_ref[...] = gap * gap * inv

            def row(r, _):
                x = out_ref[r, :, at]
                cov = jnp.dot(ybt_ref[...], anomalies(x), preferred_element_type=jnp.float32)
                near = near_ref[r]
                near = jnp.concatenate([near] * groups, axis=1)
                w = jnp.maximum(near - across_ref[...], 0.0)
                gain = (w * w * cov).astype(jnp.bfloat16)
                out_ref[r, :, at] = x + jnp.dot(dy_ref[...], gain, preferred_element_type=jnp.float32)
                return 0

            lax.fori_loop(0, rows, row, 0)
            return 0

        lax.fori_loop(0, cols // TILE, column, 0)

        def later(t, _):
            at = pl.ds(pl.multiple_of(t * TILE, TILE), TILE)
            y = y_ref[:, at]
            cov = jnp.dot(ybt_ref[...], anomalies(y), preferred_element_type=jnp.float32)
            gap_r = prow_ref[0:1, at] - pcol_ref[own, 0:1]
            gap_c = prow_ref[1:2, at] - pcol_ref[own, 1:2]
            w = jnp.maximum(q_ref[:, 0:1] - (gap_r * gap_r + gap_c * gap_c) * q_ref[:, 1:2], 0.0)
            gain = (w * w * cov).astype(jnp.bfloat16)
            y_ref[:, at] = y + jnp.dot(dy_ref[...], gain, preferred_element_type=jnp.float32)
            return 0

        per = BLK // TILE
        lax.fori_loop((b + 1) * per, NBLK * per, later, 0)
        return 0

    lax.fori_loop(0, NBLK, block, 0)


def on_device(prior, coef, observations, obs_variance, obs_row, obs_col, obs_radius, block_order):
    n_member = lax.axis_size("member")
    n_state = lax.axis_size("state")
    local_members, local_rows, cols = prior.shape
    members = local_members * n_member
    n_obs = block_order.shape[0]
    f32 = jnp.float32
    table = jnp.stack(
        [
            obs_row.astype(f32),
            obs_col.astype(f32),
            obs_radius.astype(f32),
            observations,
            obs_variance,
        ]
        + [jnp.zeros((n_obs,), f32)] * 3,
        axis=1,
    )
    by_obs = jnp.take(table, block_order, axis=0)
    by_field = by_obs.T
    row_i = by_field[0].astype(jnp.int32)
    col_i = by_field[1].astype(jnp.int32)

    now = forecast(prior, coef).transpose(1, 0, 2)
    base_row = lax.axis_index("state") * local_rows
    tile_rows = local_rows // n_member
    first_row = base_row + lax.axis_index("member") * tile_rows
    cells = lax.all_to_all(now, "member", split_axis=0, concat_axis=1, tiled=True)

    part = pl.pallas_call(
        pick_kernel,
        out_shape=jax.ShapeDtypeStruct((local_members, n_obs), f32),
        in_specs=[SMEM, SMEM, SMEM, VMEM],
        out_specs=VMEM,
        compiler_params=pltpu.CompilerParams(vmem_limit_bytes=32 * 1024 * 1024),
        cost_estimate=pl.CostEstimate(flops=10**7, bytes_accessed=10**7, transcendentals=0),
    )(jnp.reshape(base_row, (1,)).astype(jnp.int32), row_i, col_i, now)
    shared = pl.pallas_call(
        functools.partial(share_kernel, n_member, n_state),
        out_shape=jax.ShapeDtypeStruct((n_member, local_members, n_obs), f32),
        in_specs=[VMEM],
        out_specs=VMEM,
        scratch_shapes=[
            pltpu.VMEM((n_state - 1, local_members, n_obs), f32),
            pltpu.SemaphoreType.DMA((n_state - 1,)),
            pltpu.SemaphoreType.DMA((n_state - 1,)),
            pltpu.SemaphoreType.DMA((n_member - 1,)),
            pltpu.SemaphoreType.DMA((n_member - 1,)),
        ],
        compiler_params=pltpu.CompilerParams(
            collective_id=0, has_side_effects=True, vmem_limit_bytes=32 * 1024 * 1024
        ),
    )(part)
    y0 = shared.reshape(members, n_obs)
    result = pl.pallas_call(
        assimilate_kernel,
        out_shape=jax.ShapeDtypeStruct(cells.shape, f32),
        in_specs=[SMEM, VMEM, VMEM, VMEM, VMEM],
        out_specs=VMEM,
        scratch_shapes=[
            pltpu.VMEM((members, n_obs), f32),
            pltpu.VMEM((tile_rows, BLK, LANES), f32),
            pltpu.VMEM((BLK, TILE), f32),
            pltpu.VMEM((BLK, members), jnp.bfloat16),
            pltpu.VMEM((members, BLK), jnp.bfloat16),
            pltpu.VMEM((BLK, LANES), f32),
        ],
        compiler_params=pltpu.CompilerParams(vmem_limit_bytes=48 * 1024 * 1024),
    )(jnp.reshape(first_row, (1,)).astype(jnp.int32), cells, y0, by_obs, by_field)
    back = lax.all_to_all(result, "member", split_axis=1, concat_axis=0, tiled=True)
    return back.transpose(1, 0, 2)


def solution(mesh):
    in_specs = (P("member", "state", None), P("state", None), P(), P(), P(), P(), P(), P())
    out_specs = P("member", "state", None)
    return jax.shard_map(
        on_device, mesh=mesh, in_specs=in_specs, out_specs=out_specs, check_vma=False
    )
```

```python
import functools

import jax
import jax.numpy as jnp
from jax import lax
from jax.experimental import pallas as pl
from jax.experimental.pallas import tpu as pltpu
from jax.sharding import PartitionSpec as P

BLK = 512
NBLK = 6
LANES = 128
TILE = 256
PARTS = 2
EPS = 1e-06
MESH = pl.DeviceIdType.MESH
VMEM = pl.BlockSpec(memory_space=pltpu.VMEM)
SMEM = pl.BlockSpec(memory_space=pltpu.SMEM)


def forecast(u, coef):
    peers = lax.axis_size("state")
    up = [(i, i + 1) for i in range(peers - 1)]
    down = [(j, i) for i, j in up]
    rows = u.shape[1]
    last = jnp.concatenate([u[:, rows - 2 :], coef[None, rows - 2 :]], axis=0)
    first = jnp.concatenate([u[:, :2], coef[None, :2]], axis=0)
    before = lax.ppermute(last, "state", up)
    after = lax.ppermute(first, "state", down)
    current = jnp.concatenate([before[:-1], u, after[:-1]], axis=1)
    field = jnp.concatenate([before[-1], coef, after[-1]], axis=0)
    for _ in range(2):
        center = current[:, 1:-1]
        field = field[1:-1]
        vertical = current[:, 2:] + current[:, :-2]
        sideways = jnp.pad(center[:, :, 1:], ((0, 0), (0, 0), (0, 1))) + jnp.pad(
            center[:, :, :-1], ((0, 0), (0, 0), (1, 0))
        )
        current = center + field * (vertical + sideways - 4.0 * center)
    return current


def pick_kernel(where_ref, lane_ref, field_ref, out_ref):
    members = field_ref.shape[1]
    lane = lax.broadcasted_iota(jnp.int32, (members, LANES), 1)

    def chunk(j, _):
        def step(t, acc):
            for i in range(16):
                k = j * LANES + t * 16 + i
                packed = where_ref[k]
                local = lax.shift_right_logical(packed, 15)
                start = pl.multiple_of(packed & 0x7F80, LANES)
                part = field_ref[local, :, pl.ds(start, LANES)]
                turned = pltpu.roll(part, packed & (LANES - 1), 1)
                acc = jnp.where(lane == lane_ref[k], turned, acc)
            return acc

        acc = lax.fori_loop(0, LANES // 16, step, jnp.zeros((members, LANES), jnp.float32))
        out_ref[:, pl.ds(pl.multiple_of(j * LANES, LANES), LANES)] = acc
        return 0

    lax.fori_loop(0, out_ref.shape[1] // LANES, chunk, 0)


def share_kernel(n_member, n_state, part_ref, out_ref, slots, send_s, recv_s, send_m, recv_m):
    mi = lax.axis_index("member")
    si = lax.axis_index("state")
    barrier = pltpu.get_barrier_semaphore()
    for d in range(1, n_state):
        peer = lax.rem(si + d, n_state)
        pl.semaphore_signal(barrier, inc=1, device_id=(mi, peer), device_id_type=MESH)
    for d in range(1, n_member):
        peer = lax.rem(mi + d, n_member)
        pl.semaphore_signal(barrier, inc=1, device_id=(peer, si), device_id_type=MESH)
    pl.semaphore_wait(barrier, n_state + n_member - 2)
    first = []
    for d in range(1, n_state):
        peer = lax.rem(si + d, n_state)
        copy = pltpu.make_async_remote_copy(
            src_ref=part_ref,
            dst_ref=slots.at[d - 1],
            send_sem=send_s.at[d - 1],
            recv_sem=recv_s.at[d - 1],
            device_id=(mi, peer),
            device_id_type=MESH,
        )
        copy.start()
        first.append(copy)
    total = part_ref[...]
    for d in range(1, n_state):
        first[d - 1].wait()
        total = total + slots[d - 1]
    out_ref[mi] = total
    second = []
    for d in range(1, n_member):
        peer = lax.rem(mi + d, n_member)
        copy = pltpu.make_async_remote_copy(
            src_ref=out_ref.at[mi],
            dst_ref=out_ref.at[mi],
            send_sem=send_m.at[d - 1],
            recv_sem=recv_m.at[d - 1],
            device_id=(peer, si),
            device_id_type=MESH,
        )
        copy.start()
        second.append(copy)
    for copy in second:
        copy.wait()


def anomalies(values):
    return (values - jnp.mean(values, axis=0, keepdims=True)).astype(jnp.bfloat16)


def observed_kernel(y0_ref, pcol_ref, prow_ref, ybt_ref, dy_ref, q_ref, y_ref):
    members = y0_ref.shape[0]
    y_ref[...] = y0_ref[...]

    def block(b, _):
        own = pl.ds(pl.multiple_of(b * BLK, BLK), BLK)
        values = y_ref[:, own]
        mean = jnp.mean(values, axis=0, keepdims=True)
        anomaly = values - mean
        spread = jnp.sum(anomaly * anomaly, axis=0, keepdims=True) / (members - 1) + EPS
        observed = prow_ref[3:4, own]
        variance = prow_ref[4:5, own]
        post = spread * variance / (spread + variance)
        center = post * (mean / spread + observed / variance)
        shrink = jnp.sqrt(variance / (variance + spread)) - 1.0
        dy_ref[:, own] = (center - mean + shrink * anomaly).astype(jnp.bfloat16)
        turned = anomaly.T
        ybt_ref[own, :] = turned.astype(jnp.bfloat16)
        spread_c = jnp.sum(turned * turned, axis=1, keepdims=True) / (members - 1) + EPS
        q = jnp.sqrt(1.0 / (spread_c * (members - 1)))
        reach = pcol_ref[own, 2:3]
        q_ref[own, 0:1] = q
        q_ref[own, 1:2] = q / (reach * reach)

        def later(t, _):
            at = pl.ds(pl.multiple_of(t * TILE, TILE), TILE)
            y = y_ref[:, at]
            cov = jnp.dot(ybt_ref[own, :], anomalies(y), preferred_element_type=jnp.float32)
            gap_r = prow_ref[0:1, at] - pcol_ref[own, 0:1]
            gap_c = prow_ref[1:2, at] - pcol_ref[own, 1:2]
            far = (gap_r * gap_r + gap_c * gap_c) * q_ref[own, 1:2]
            w = jnp.maximum(q_ref[own, 0:1] - far, 0.0)
            gain = (w * w * cov).astype(jnp.bfloat16)
            y_ref[:, at] = y + jnp.dot(dy_ref[:, own], gain, preferred_element_type=jnp.float32)
            return 0

        per = BLK // TILE
        lax.fori_loop((b + 1) * per, NBLK * per, later, 0)
        return 0

    lax.fori_loop(0, NBLK, block, 0)


def cells_kernel(
    first_col, base_ref, x_ref, pcol_ref, ybt_ref, dy_ref, q_ref, out_ref, near_ref, across_ref
):
    rows, members, cols = x_ref.shape
    base = base_ref[0].astype(jnp.float32)
    out_ref[...] = x_ref[...]
    groups = TILE // LANES
    together = 4 if rows % 4 == 0 else 1

    def block(b, _):
        own = pl.ds(pl.multiple_of(b * BLK, BLK), BLK)
        obs_r = pcol_ref[own, 0:1]
        obs_c = pcol_ref[own, 1:2]
        q = q_ref[own, 0:1]
        inv = q_ref[own, 1:2]
        for r in range(rows):
            gap = base + float(r) - obs_r
            near_ref[r] = jnp.broadcast_to(q - gap * gap * inv, (BLK, LANES))

        def column(t, _):
            at = pl.ds(pl.multiple_of(t * TILE, TILE), TILE)
            place = lax.broadcasted_iota(jnp.int32, (1, TILE), 1) + (t * TILE + first_col)
            gap = place.astype(jnp.float32) - obs_c
            across_ref[...] = gap * gap * inv

            def row(g, _):
                xs = [out_ref[g * together + i, :, at] for i in range(together)]
                news = []
                for i in range(together):
                    cov = jnp.dot(
                        ybt_ref[own, :], anomalies(xs[i]), preferred_element_type=jnp.float32
                    )
                    near = jnp.concatenate([near_ref[g * together + i]] * groups, axis=1)
                    w = jnp.maximum(near - across_ref[...], 0.0)
                    gain = (w * w * cov).astype(jnp.bfloat16)
                    news.append(
                        xs[i] + jnp.dot(dy_ref[:, own], gain, preferred_element_type=jnp.float32)
                    )
                for i in range(together):
                    out_ref[g * together + i, :, at] = news[i]
                return 0

            lax.fori_loop(0, rows // together, row, 0)
            return 0

        lax.fori_loop(0, cols // TILE, column, 0)
        return 0

    lax.fori_loop(0, NBLK, block, 0)


def on_device(prior, coef, observations, obs_variance, obs_row, obs_col, obs_radius, block_order):
    n_member = lax.axis_size("member")
    n_state = lax.axis_size("state")
    local_members, local_rows, cols = prior.shape
    members = local_members * n_member
    n_obs = block_order.shape[0]
    f32 = jnp.float32
    table = jnp.stack(
        [
            obs_row.astype(f32),
            obs_col.astype(f32),
            obs_radius.astype(f32),
            observations,
            obs_variance,
        ]
        + [jnp.zeros((n_obs,), f32)] * 3,
        axis=1,
    )
    by_obs = jnp.take(table, block_order, axis=0)
    by_field = by_obs.T
    row_i = by_field[0].astype(jnp.int32)
    col_i = by_field[1].astype(jnp.int32)

    now = forecast(prior, coef).transpose(1, 0, 2)
    base_row = lax.axis_index("state") * local_rows
    tile_rows = local_rows // n_member
    first_row = base_row + lax.axis_index("member") * tile_rows
    width = cols // PARTS
    cells = [
        lax.all_to_all(
            now[:, :, p * width : (p + 1) * width], "member", split_axis=0, concat_axis=1, tiled=True
        )
        for p in range(PARTS)
    ]

    local = row_i - base_row
    inside = (local >= 0) & (local < local_rows)
    index = jnp.arange(n_obs, dtype=jnp.int32)
    turn = (index - col_i) & (LANES - 1)
    packed = (jnp.where(inside, local, 0) << 15) | (col_i & 0x7F80) | turn
    target = jnp.where(inside, index & (LANES - 1), -1)
    part = pl.pallas_call(
        pick_kernel,
        out_shape=jax.ShapeDtypeStruct((local_members, n_obs), f32),
        in_specs=[SMEM, SMEM, VMEM],
        out_specs=VMEM,
        compiler_params=pltpu.CompilerParams(vmem_limit_bytes=32 * 1024 * 1024),
        cost_estimate=pl.CostEstimate(flops=10**7, bytes_accessed=10**7, transcendentals=0),
    )(packed, target, now)
    shared = pl.pallas_call(
        functools.partial(share_kernel, n_member, n_state),
        out_shape=jax.ShapeDtypeStruct((n_member, local_members, n_obs), f32),
        in_specs=[VMEM],
        out_specs=VMEM,
        scratch_shapes=[
            pltpu.VMEM((n_state - 1, local_members, n_obs), f32),
            pltpu.SemaphoreType.DMA((n_state - 1,)),
            pltpu.SemaphoreType.DMA((n_state - 1,)),
            pltpu.SemaphoreType.DMA((n_member - 1,)),
            pltpu.SemaphoreType.DMA((n_member - 1,)),
        ],
        compiler_params=pltpu.CompilerParams(
            collective_id=0, has_side_effects=True, vmem_limit_bytes=32 * 1024 * 1024
        ),
    )(part)
    y0 = shared.reshape(members, n_obs)
    ybt, dy, q = pl.pallas_call(
        observed_kernel,
        out_shape=[
            jax.ShapeDtypeStruct((n_obs, members), jnp.bfloat16),
            jax.ShapeDtypeStruct((members, n_obs), jnp.bfloat16),
            jax.ShapeDtypeStruct((n_obs, 8), f32),
        ],
        in_specs=[VMEM] * 3,
        out_specs=[VMEM] * 3,
        scratch_shapes=[pltpu.VMEM((members, n_obs), f32)],
        compiler_params=pltpu.CompilerParams(vmem_limit_bytes=40 * 1024 * 1024),
        cost_estimate=pl.CostEstimate(flops=10**9, bytes_accessed=10**7, transcendentals=0),
    )(y0, by_obs, by_field)
    backs = []
    for p in range(PARTS):
        result = pl.pallas_call(
            functools.partial(cells_kernel, p * width),
            out_shape=jax.ShapeDtypeStruct(cells[p].shape, f32),
            in_specs=[SMEM] + [VMEM] * 5,
            out_specs=VMEM,
            scratch_shapes=[
                pltpu.VMEM((tile_rows, BLK, LANES), f32),
                pltpu.VMEM((BLK, TILE), f32),
            ],
            compiler_params=pltpu.CompilerParams(vmem_limit_bytes=40 * 1024 * 1024),
            cost_estimate=pl.CostEstimate(
                flops=2 * 10**10, bytes_accessed=10**7, transcendentals=0
            ),
        )(jnp.reshape(first_row, (1,)).astype(jnp.int32), cells[p], by_obs, ybt, dy, q)
        backs.append(
            lax.all_to_all(result, "member", split_axis=1, concat_axis=0, tiled=True)
        )
    return jnp.concatenate([back.transpose(1, 0, 2) for back in backs], axis=2)


def solution(mesh):
    in_specs = (P("member", "state", None), P("state", None), P(), P(), P(), P(), P(), P())
    out_specs = P("member", "state", None)
    return jax.shard_map(
        on_device, mesh=mesh, in_specs=in_specs, out_specs=out_specs, check_vma=False
    )
```

```python
import functools

import jax
import jax.numpy as jnp
from jax import lax
from jax.experimental import pallas as pl
from jax.experimental.pallas import tpu as pltpu
from jax.sharding import PartitionSpec as P

BLK = 512
NBLK = 6
LANES = 128
TILE = 256
PARTS = 2
EPS = 1e-06
MESH = pl.DeviceIdType.MESH
VMEM = pl.BlockSpec(memory_space=pltpu.VMEM)
SMEM = pl.BlockSpec(memory_space=pltpu.SMEM)


def forecast(u, coef):
    peers = lax.axis_size("state")
    up = [(i, i + 1) for i in range(peers - 1)]
    down = [(j, i) for i, j in up]
    rows = u.shape[1]
    last = jnp.concatenate([u[:, rows - 2 :], coef[None, rows - 2 :]], axis=0)
    first = jnp.concatenate([u[:, :2], coef[None, :2]], axis=0)
    before = lax.ppermute(last, "state", up)
    after = lax.ppermute(first, "state", down)
    current = jnp.concatenate([before[:-1], u, after[:-1]], axis=1)
    field = jnp.concatenate([before[-1], coef, after[-1]], axis=0)
    for _ in range(2):
        center = current[:, 1:-1]
        field = field[1:-1]
        vertical = current[:, 2:] + current[:, :-2]
        sideways = jnp.pad(center[:, :, 1:], ((0, 0), (0, 0), (0, 1))) + jnp.pad(
            center[:, :, :-1], ((0, 0), (0, 0), (1, 0))
        )
        current = center + field * (vertical + sideways - 4.0 * center)
    return current


def pick_kernel(where_ref, lane_ref, field_ref, out_ref):
    members = field_ref.shape[1]
    lane = lax.broadcasted_iota(jnp.int32, (members, LANES), 1)

    def chunk(j, _):
        def step(t, acc):
            for i in range(16):
                k = j * LANES + t * 16 + i
                packed = where_ref[k]
                local = lax.shift_right_logical(packed, 15)
                start = pl.multiple_of(packed & 0x7F80, LANES)
                part = field_ref[local, :, pl.ds(start, LANES)]
                turned = pltpu.roll(part, packed & (LANES - 1), 1)
                acc = jnp.where(lane == lane_ref[k], turned, acc)
            return acc

        acc = lax.fori_loop(0, LANES // 16, step, jnp.zeros((members, LANES), jnp.float32))
        out_ref[:, pl.ds(pl.multiple_of(j * LANES, LANES), LANES)] = acc
        return 0

    lax.fori_loop(0, out_ref.shape[1] // LANES, chunk, 0)


def share_kernel(n_member, n_state, part_ref, out_ref, slots, send_s, recv_s, send_m, recv_m):
    mi = lax.axis_index("member")
    si = lax.axis_index("state")
    barrier = pltpu.get_barrier_semaphore()
    for d in range(1, n_state):
        peer = lax.rem(si + d, n_state)
        pl.semaphore_signal(barrier, inc=1, device_id=(mi, peer), device_id_type=MESH)
    for d in range(1, n_member):
        peer = lax.rem(mi + d, n_member)
        pl.semaphore_signal(barrier, inc=1, device_id=(peer, si), device_id_type=MESH)
    pl.semaphore_wait(barrier, n_state + n_member - 2)
    first = []
    for d in range(1, n_state):
        peer = lax.rem(si + d, n_state)
        copy = pltpu.make_async_remote_copy(
            src_ref=part_ref,
            dst_ref=slots.at[d - 1],
            send_sem=send_s.at[d - 1],
            recv_sem=recv_s.at[d - 1],
            device_id=(mi, peer),
            device_id_type=MESH,
        )
        copy.start()
        first.append(copy)
    total = part_ref[...]
    for d in range(1, n_state):
        first[d - 1].wait()
        total = total + slots[d - 1]
    out_ref[mi] = total
    second = []
    for d in range(1, n_member):
        peer = lax.rem(mi + d, n_member)
        copy = pltpu.make_async_remote_copy(
            src_ref=out_ref.at[mi],
            dst_ref=out_ref.at[mi],
            send_sem=send_m.at[d - 1],
            recv_sem=recv_m.at[d - 1],
            device_id=(peer, si),
            device_id_type=MESH,
        )
        copy.start()
        second.append(copy)
    for copy in second:
        copy.wait()


def anomalies(values):
    return (values - jnp.mean(values, axis=0, keepdims=True)).astype(jnp.bfloat16)


def observed_kernel(y0_ref, pcol_ref, prow_ref, ybt_ref, dy_ref, q_ref, y_ref):
    members = y0_ref.shape[0]
    y_ref[...] = y0_ref[...]

    def block(b, _):
        own = pl.ds(pl.multiple_of(b * BLK, BLK), BLK)
        values = y_ref[:, own]
        mean = jnp.mean(values, axis=0, keepdims=True)
        anomaly = values - mean
        spread = jnp.sum(anomaly * anomaly, axis=0, keepdims=True) / (members - 1) + EPS
        observed = prow_ref[3:4, own]
        variance = prow_ref[4:5, own]
        post = spread * variance / (spread + variance)
        center = post * (mean / spread + observed / variance)
        shrink = jnp.sqrt(variance / (variance + spread)) - 1.0
        dy_ref[:, own] = (center - mean + shrink * anomaly).astype(jnp.bfloat16)
        turned = anomaly.T
        ybt_ref[own, :] = turned.astype(jnp.bfloat16)
        spread_c = jnp.sum(turned * turned, axis=1, keepdims=True) / (members - 1) + EPS
        q = jnp.sqrt(1.0 / (spread_c * (members - 1)))
        reach = pcol_ref[own, 2:3]
        q_ref[own, 0:1] = q
        q_ref[own, 1:2] = q / (reach * reach)

        def later(t, _):
            at = pl.ds(pl.multiple_of(t * TILE, TILE), TILE)
            y = y_ref[:, at]
            cov = jnp.dot(ybt_ref[own, :], anomalies(y), preferred_element_type=jnp.float32)
            gap_r = prow_ref[0:1, at] - pcol_ref[own, 0:1]
            gap_c = prow_ref[1:2, at] - pcol_ref[own, 1:2]
            far = (gap_r * gap_r + gap_c * gap_c) * q_ref[own, 1:2]
            w = jnp.maximum(q_ref[own, 0:1] - far, 0.0)
            gain = (w * w * cov).astype(jnp.bfloat16)
            y_ref[:, at] = y + jnp.dot(dy_ref[:, own], gain, preferred_element_type=jnp.float32)
            return 0

        per = BLK // TILE
        lax.fori_loop((b + 1) * per, NBLK * per, later, 0)
        return 0

    lax.fori_loop(0, NBLK, block, 0)


def cells_kernel(
    n_tiles, first_col, base_ref, span_ref, x_ref, pcol_ref, ybt_ref, dy_ref, q_ref, out_ref, near_ref, across_ref
):
    rows, members, cols = x_ref.shape
    base = base_ref[0].astype(jnp.float32)
    out_ref[...] = x_ref[...]
    groups = TILE // LANES
    together = 4 if rows % 4 == 0 else 1

    def block(b, _):
        own = pl.ds(pl.multiple_of(b * BLK, BLK), BLK)
        obs_r = pcol_ref[own, 0:1]
        q = q_ref[own, 0:1]
        inv = q_ref[own, 1:2]
        for r in range(rows):
            gap = base + float(r) - obs_r
            near_ref[r] = jnp.broadcast_to(q - gap * gap * inv, (BLK, LANES))

        def column(t, _):
            at = pl.ds(pl.multiple_of(t * TILE, TILE), TILE)
            place = lax.broadcasted_iota(jnp.int32, (1, TILE), 1) + (t * TILE + first_col)
            place = place.astype(jnp.float32)
            entry = (b * n_tiles + first_col // TILE + t) * 2
            lead = span_ref[entry] * LANES
            count = span_ref[entry + 1]

            def window(size):
                mine = pl.ds(pl.multiple_of(lead, LANES), size)
                ours = pl.ds(pl.multiple_of(b * BLK + lead, LANES), size)
                gap = place - pcol_ref[ours, 1:2]
                across_ref[0:size, :] = gap * gap * q_ref[ours, 1:2]

                def row(g, _):
                    xs = [out_ref[g * together + i, :, at] for i in range(together)]
                    news = []
                    for i in range(together):
                        cov = jnp.dot(
                            ybt_ref[ours, :], anomalies(xs[i]), preferred_element_type=jnp.float32
                        )
                        near = jnp.concatenate([near_ref[g * together + i, mine, :]] * groups, axis=1)
                        w = jnp.maximum(near - across_ref[0:size, :], 0.0)
                        gain = (w * w * cov).astype(jnp.bfloat16)
                        news.append(
                            xs[i]
                            + jnp.dot(dy_ref[:, ours], gain, preferred_element_type=jnp.float32)
                        )
                    for i in range(together):
                        out_ref[g * together + i, :, at] = news[i]
                    return 0

                lax.fori_loop(0, rows // together, row, 0)

            for parts in range(1, BLK // LANES + 1):
                pl.when(count == parts)(functools.partial(window, parts * LANES))
            return 0

        lax.fori_loop(0, cols // TILE, column, 0)
        return 0

    lax.fori_loop(0, NBLK, block, 0)


def by_column(table, reach, cols):
    blocks = table.reshape(NBLK, BLK, table.shape[1])
    key = blocks[:, :, 1].astype(jnp.int32) * BLK + jnp.arange(BLK, dtype=jnp.int32)
    rank = jnp.sum((key[:, None, :] < key[:, :, None]).astype(jnp.int32), axis=2)
    chosen = (jnp.arange(BLK, dtype=jnp.int32)[None, :, None] == rank[:, None, :]).astype(jnp.float32)
    ordered = jnp.einsum("bpi,bif->bpf", chosen, blocks, precision=lax.Precision.HIGHEST)
    column = blocks[:, None, :, 1].astype(jnp.int32)
    start = (jnp.arange(cols // TILE, dtype=jnp.int32) * TILE)[None, :, None]
    before = jnp.sum((column < start - reach).astype(jnp.int32), axis=2)
    until = jnp.sum((column < start + TILE + reach).astype(jnp.int32), axis=2)
    lead = jnp.minimum(before // LANES, BLK // LANES - 1)
    count = jnp.maximum((until + LANES - 1) // LANES - lead, 0)
    return ordered.reshape(table.shape), jnp.stack([lead, count], axis=-1).reshape(-1)


def on_device(prior, coef, observations, obs_variance, obs_row, obs_col, obs_radius, block_order):
    n_member = lax.axis_size("member")
    n_state = lax.axis_size("state")
    local_members, local_rows, cols = prior.shape
    members = local_members * n_member
    n_obs = block_order.shape[0]
    f32 = jnp.float32
    table = jnp.stack(
        [
            obs_row.astype(f32),
            obs_col.astype(f32),
            obs_radius.astype(f32),
            observations,
            obs_variance,
        ]
        + [jnp.zeros((n_obs,), f32)] * 3,
        axis=1,
    )
    by_obs, span = by_column(jnp.take(table, block_order, axis=0), jnp.max(obs_radius), cols)
    by_field = by_obs.T
    row_i = by_field[0].astype(jnp.int32)
    col_i = by_field[1].astype(jnp.int32)

    now = forecast(prior, coef).transpose(1, 0, 2)
    base_row = lax.axis_index("state") * local_rows
    tile_rows = local_rows // n_member
    first_row = base_row + lax.axis_index("member") * tile_rows
    width = cols // PARTS
    cells = [
        lax.all_to_all(
            now[:, :, p * width : (p + 1) * width], "member", split_axis=0, concat_axis=1, tiled=True
        )
        for p in range(PARTS)
    ]

    local = row_i - base_row
    inside = (local >= 0) & (local < local_rows)
    index = jnp.arange(n_obs, dtype=jnp.int32)
    turn = (index - col_i) & (LANES - 1)
    packed = (jnp.where(inside, local, 0) << 15) | (col_i & 0x7F80) | turn
    target = jnp.where(inside, index & (LANES - 1), -1)
    part = pl.pallas_call(
        pick_kernel,
        out_shape=jax.ShapeDtypeStruct((local_members, n_obs), f32),
        in_specs=[SMEM, SMEM, VMEM],
        out_specs=VMEM,
        compiler_params=pltpu.CompilerParams(vmem_limit_bytes=32 * 1024 * 1024),
        cost_estimate=pl.CostEstimate(flops=10**7, bytes_accessed=10**7, transcendentals=0),
    )(packed, target, now)
    shared = pl.pallas_call(
        functools.partial(share_kernel, n_member, n_state),
        out_shape=jax.ShapeDtypeStruct((n_member, local_members, n_obs), f32),
        in_specs=[VMEM],
        out_specs=VMEM,
        scratch_shapes=[
            pltpu.VMEM((n_state - 1, local_members, n_obs), f32),
            pltpu.SemaphoreType.DMA((n_state - 1,)),
            pltpu.SemaphoreType.DMA((n_state - 1,)),
            pltpu.SemaphoreType.DMA((n_member - 1,)),
            pltpu.SemaphoreType.DMA((n_member - 1,)),
        ],
        compiler_params=pltpu.CompilerParams(
            collective_id=0, has_side_effects=True, vmem_limit_bytes=32 * 1024 * 1024
        ),
    )(part)
    y0 = shared.reshape(members, n_obs)
    ybt, dy, q = pl.pallas_call(
        observed_kernel,
        out_shape=[
            jax.ShapeDtypeStruct((n_obs, members), jnp.bfloat16),
            jax.ShapeDtypeStruct((members, n_obs), jnp.bfloat16),
            jax.ShapeDtypeStruct((n_obs, 8), f32),
        ],
        in_specs=[VMEM] * 3,
        out_specs=[VMEM] * 3,
        scratch_shapes=[pltpu.VMEM((members, n_obs), f32)],
        compiler_params=pltpu.CompilerParams(vmem_limit_bytes=40 * 1024 * 1024),
        cost_estimate=pl.CostEstimate(flops=10**9, bytes_accessed=10**7, transcendentals=0),
    )(y0, by_obs, by_field)
    backs = []
    for p in range(PARTS):
        result = pl.pallas_call(
            functools.partial(cells_kernel, cols // TILE, p * width),
            out_shape=jax.ShapeDtypeStruct(cells[p].shape, f32),
            in_specs=[SMEM, SMEM] + [VMEM] * 5,
            out_specs=VMEM,
            scratch_shapes=[
                pltpu.VMEM((tile_rows, BLK, LANES), f32),
                pltpu.VMEM((BLK, TILE), f32),
            ],
            compiler_params=pltpu.CompilerParams(vmem_limit_bytes=40 * 1024 * 1024),
            cost_estimate=pl.CostEstimate(
                flops=2 * 10**10, bytes_accessed=10**7, transcendentals=0
            ),
        )(jnp.reshape(first_row, (1,)).astype(jnp.int32), span, cells[p], by_obs, ybt, dy, q)
        backs.append(
            lax.all_to_all(result, "member", split_axis=1, concat_axis=0, tiled=True)
        )
    return jnp.concatenate([back.transpose(1, 0, 2) for back in backs], axis=2)


def solution(mesh):
    in_specs = (P("member", "state", None), P("state", None), P(), P(), P(), P(), P(), P())
    out_specs = P("member", "state", None)
    return jax.shard_map(
        on_device, mesh=mesh, in_specs=in_specs, out_specs=out_specs, check_vma=False
    )
```

```python
import functools

import jax
import jax.numpy as jnp
from jax import lax
from jax.experimental import pallas as pl
from jax.experimental.pallas import tpu as pltpu
from jax.sharding import PartitionSpec as P

BLK = 512
NBLK = 6
LANES = 128
TILE = 256
PARTS = 2
EPS = 1e-06
MESH = pl.DeviceIdType.MESH
VMEM = pl.BlockSpec(memory_space=pltpu.VMEM)
SMEM = pl.BlockSpec(memory_space=pltpu.SMEM)


def forecast(u, coef):
    peers = lax.axis_size("state")
    up = [(i, i + 1) for i in range(peers - 1)]
    down = [(j, i) for i, j in up]
    rows = u.shape[1]
    last = jnp.concatenate([u[:, rows - 2 :], coef[None, rows - 2 :]], axis=0)
    first = jnp.concatenate([u[:, :2], coef[None, :2]], axis=0)
    before = lax.ppermute(last, "state", up)
    after = lax.ppermute(first, "state", down)
    current = jnp.concatenate([before[:-1], u, after[:-1]], axis=1)
    field = jnp.concatenate([before[-1], coef, after[-1]], axis=0)
    for _ in range(2):
        center = current[:, 1:-1]
        field = field[1:-1]
        vertical = current[:, 2:] + current[:, :-2]
        sideways = jnp.pad(center[:, :, 1:], ((0, 0), (0, 0), (0, 1))) + jnp.pad(
            center[:, :, :-1], ((0, 0), (0, 0), (1, 0))
        )
        current = center + field * (vertical + sideways - 4.0 * center)
    return current


def pick_kernel(where_ref, lane_ref, field_ref, out_ref):
    members = field_ref.shape[1]
    lane = lax.broadcasted_iota(jnp.int32, (members, LANES), 1)

    def chunk(j, _):
        def step(t, acc):
            for i in range(16):
                k = j * LANES + t * 16 + i
                packed = where_ref[k]
                local = lax.shift_right_logical(packed, 15)
                start = pl.multiple_of(packed & 0x7F80, LANES)
                part = field_ref[local, :, pl.ds(start, LANES)]
                turned = pltpu.roll(part, packed & (LANES - 1), 1)
                acc = jnp.where(lane == lane_ref[k], turned, acc)
            return acc

        acc = lax.fori_loop(0, LANES // 16, step, jnp.zeros((members, LANES), jnp.float32))
        out_ref[:, pl.ds(pl.multiple_of(j * LANES, LANES), LANES)] = acc
        return 0

    lax.fori_loop(0, out_ref.shape[1] // LANES, chunk, 0)


def share_kernel(
    n_z, n_state, part_ref, out_ref, slots, send_1, recv_1, send_2, recv_2, send_3, recv_3, send_4, recv_4
):
    mi = lax.axis_index("member")
    si = lax.axis_index("state")
    core = lax.rem(mi, 2)
    z = lax.div(mi, 2)
    sibling = (z * 2 + 1 - core, si)
    across = [(mi, lax.rem(si + d, n_state)) for d in range(1, n_state)]
    along = [(lax.rem(z + d, n_z) * 2 + core, si) for d in range(1, n_z)]
    barrier = pltpu.get_barrier_semaphore()
    for peer in across + along + [sibling]:
        pl.semaphore_signal(barrier, inc=1, device_id=peer, device_id_type=MESH)
    pl.semaphore_wait(barrier, n_state + n_z - 1)

    def send(source, target, send_sem, recv_sem, peer):
        copy = pltpu.make_async_remote_copy(
            src_ref=source,
            dst_ref=target,
            send_sem=send_sem,
            recv_sem=recv_sem,
            device_id=peer,
            device_id_type=MESH,
        )
        copy.start()
        return copy

    first = [
        send(part_ref.at[peer[1]], slots.at[d], send_1.at[d], recv_1.at[d], peer)
        for d, peer in enumerate(across)
    ]
    total = part_ref[si]
    for d in range(n_state - 1):
        first[d].wait()
        total = total + slots[d]
    out_ref[core, si, z] = total
    mine = out_ref.at[core, si, z]
    second = [
        send(mine, mine, send_2.at[d], recv_2.at[d], peer) for d, peer in enumerate(along)
    ]
    for copy in second:
        copy.wait()
    line = out_ref.at[core, si]
    third = [
        send(line, line, send_3.at[d], recv_3.at[d], peer) for d, peer in enumerate(across)
    ]
    last = [send(line, line, send_4.at[0], recv_4.at[0], sibling)]
    for d in range(1, n_state):
        third[d - 1].wait()
        other = out_ref.at[core, lax.rem(si + n_state - d, n_state)]
        last.append(send(other, other, send_4.at[d], recv_4.at[d], sibling))
    for copy in last:
        copy.wait()


def anomalies(values):
    return (values - jnp.mean(values, axis=0, keepdims=True)).astype(jnp.bfloat16)


def observed_kernel(y0_ref, pcol_ref, prow_ref, ybt_ref, dy_ref, q_ref, y_ref):
    members = y0_ref.shape[0]
    y_ref[...] = y0_ref[...]

    def block(b, _):
        own = pl.ds(pl.multiple_of(b * BLK, BLK), BLK)
        values = y_ref[:, own]
        mean = jnp.mean(values, axis=0, keepdims=True)
        anomaly = values - mean
        spread = jnp.sum(anomaly * anomaly, axis=0, keepdims=True) / (members - 1) + EPS
        observed = prow_ref[3:4, own]
        variance = prow_ref[4:5, own]
        post = spread * variance / (spread + variance)
        center = post * (mean / spread + observed / variance)
        shrink = jnp.sqrt(variance / (variance + spread)) - 1.0
        dy_ref[:, own] = (center - mean + shrink * anomaly).astype(jnp.bfloat16)
        turned = anomaly.T
        ybt_ref[own, :] = turned.astype(jnp.bfloat16)
        spread_c = jnp.sum(turned * turned, axis=1, keepdims=True) / (members - 1) + EPS
        q = jnp.sqrt(1.0 / (spread_c * (members - 1)))
        reach = pcol_ref[own, 2:3]
        q_ref[own, 0:1] = q
        q_ref[own, 1:2] = q / (reach * reach)

        def later(t, _):
            at = pl.ds(pl.multiple_of(t * TILE, TILE), TILE)
            y = y_ref[:, at]
            cov = jnp.dot(ybt_ref[own, :], anomalies(y), preferred_element_type=jnp.float32)
            gap_r = prow_ref[0:1, at] - pcol_ref[own, 0:1]
            gap_c = prow_ref[1:2, at] - pcol_ref[own, 1:2]
            far = (gap_r * gap_r + gap_c * gap_c) * q_ref[own, 1:2]
            w = jnp.maximum(q_ref[own, 0:1] - far, 0.0)
            gain = (w * w * cov).astype(jnp.bfloat16)
            y_ref[:, at] = y + jnp.dot(dy_ref[:, own], gain, preferred_element_type=jnp.float32)
            return 0

        per = BLK // TILE
        lax.fori_loop((b + 1) * per, NBLK * per, later, 0)
        return 0

    lax.fori_loop(0, NBLK, block, 0)


def cells_kernel(
    n_tiles, first_col, base_ref, span_ref, x_ref, pcol_ref, ybt_ref, dy_ref, q_ref, out_ref, near_ref, across_ref
):
    rows, members, cols = x_ref.shape
    base = base_ref[0].astype(jnp.float32)
    out_ref[...] = x_ref[...]
    groups = TILE // LANES
    together = 4 if rows % 4 == 0 else 1

    def block(b, _):
        own = pl.ds(pl.multiple_of(b * BLK, BLK), BLK)
        obs_r = pcol_ref[own, 0:1]
        q = q_ref[own, 0:1]
        inv = q_ref[own, 1:2]
        for r in range(rows):
            gap = base + float(r) - obs_r
            near_ref[r] = jnp.broadcast_to(q - gap * gap * inv, (BLK, LANES))

        def column(t, _):
            at = pl.ds(pl.multiple_of(t * TILE, TILE), TILE)
            place = lax.broadcasted_iota(jnp.int32, (1, TILE), 1) + (t * TILE + first_col)
            place = place.astype(jnp.float32)
            entry = (b * n_tiles + first_col // TILE + t) * 2
            lead = span_ref[entry] * LANES
            count = span_ref[entry + 1]

            def window(size):
                mine = pl.ds(pl.multiple_of(lead, LANES), size)
                ours = pl.ds(pl.multiple_of(b * BLK + lead, LANES), size)
                gap = place - pcol_ref[ours, 1:2]
                across_ref[0:size, :] = gap * gap * q_ref[ours, 1:2]

                def row(g, _):
                    xs = [out_ref[g * together + i, :, at] for i in range(together)]
                    x = jnp.concatenate(xs, axis=1)
                    cov = jnp.dot(ybt_ref[ours, :], anomalies(x), preferred_element_type=jnp.float32)
                    far = across_ref[0:size, :]
                    gains = []
                    for i in range(together):
                        near = jnp.concatenate([near_ref[g * together + i, mine, :]] * groups, axis=1)
                        w = jnp.maximum(near - far, 0.0)
                        gains.append(
                            (w * w * cov[:, i * TILE : (i + 1) * TILE]).astype(jnp.bfloat16)
                        )
                    x = x + jnp.dot(
                        dy_ref[:, ours],
                        jnp.concatenate(gains, axis=1),
                        preferred_element_type=jnp.float32,
                    )
                    for i in range(together):
                        out_ref[g * together + i, :, at] = x[:, i * TILE : (i + 1) * TILE]
                    return 0

                lax.fori_loop(0, rows // together, row, 0)

            for parts in range(1, BLK // LANES + 1):
                pl.when(count == parts)(functools.partial(window, parts * LANES))
            return 0

        lax.fori_loop(0, cols // TILE, column, 0)
        return 0

    lax.fori_loop(0, NBLK, block, 0)


def by_column(table, reach, cols):
    blocks = table.reshape(NBLK, BLK, table.shape[1])
    key = blocks[:, :, 1].astype(jnp.int32) * BLK + jnp.arange(BLK, dtype=jnp.int32)
    rank = jnp.sum((key[:, None, :] < key[:, :, None]).astype(jnp.int32), axis=2)
    chosen = (jnp.arange(BLK, dtype=jnp.int32)[None, :, None] == rank[:, None, :]).astype(jnp.float32)
    ordered = jnp.einsum("bpi,bif->bpf", chosen, blocks, precision=lax.Precision.HIGHEST)
    column = blocks[:, None, :, 1].astype(jnp.int32)
    start = (jnp.arange(cols // TILE, dtype=jnp.int32) * TILE)[None, :, None]
    before = jnp.sum((column < start - reach).astype(jnp.int32), axis=2)
    until = jnp.sum((column < start + TILE + reach).astype(jnp.int32), axis=2)
    lead = jnp.minimum(before // LANES, BLK // LANES - 1)
    count = jnp.maximum((until + LANES - 1) // LANES - lead, 0)
    return ordered.reshape(table.shape), jnp.stack([lead, count], axis=-1).reshape(-1)


def on_device(prior, coef, observations, obs_variance, obs_row, obs_col, obs_radius, block_order):
    n_member = lax.axis_size("member")
    n_state = lax.axis_size("state")
    local_members, local_rows, cols = prior.shape
    members = local_members * n_member
    n_obs = block_order.shape[0]
    f32 = jnp.float32
    table = jnp.stack(
        [
            obs_row.astype(f32),
            obs_col.astype(f32),
            obs_radius.astype(f32),
            observations,
            obs_variance,
        ]
        + [jnp.zeros((n_obs,), f32)] * 3,
        axis=1,
    )
    by_obs, span = by_column(jnp.take(table, block_order, axis=0), jnp.max(obs_radius), cols)
    by_field = by_obs.T
    row_i = by_field[0].astype(jnp.int32)
    col_i = by_field[1].astype(jnp.int32)

    now = forecast(prior, coef).transpose(1, 0, 2)
    base_row = lax.axis_index("state") * local_rows
    tile_rows = local_rows // n_member
    first_row = base_row + lax.axis_index("member") * tile_rows
    width = cols // PARTS
    cells = [
        lax.all_to_all(
            now[:, :, p * width : (p + 1) * width], "member", split_axis=0, concat_axis=1, tiled=True
        )
        for p in range(PARTS)
    ]

    local = row_i - base_row
    inside = (local >= 0) & (local < local_rows)
    index = jnp.arange(n_obs, dtype=jnp.int32)
    turn = (index - col_i) & (LANES - 1)
    packed = (jnp.where(inside, local, 0) << 15) | (col_i & 0x7F80) | turn
    target = jnp.where(inside, index & (LANES - 1), -1)
    part = pl.pallas_call(
        pick_kernel,
        out_shape=jax.ShapeDtypeStruct((local_members, n_obs), f32),
        in_specs=[SMEM, SMEM, VMEM],
        out_specs=VMEM,
        compiler_params=pltpu.CompilerParams(vmem_limit_bytes=32 * 1024 * 1024),
        cost_estimate=pl.CostEstimate(flops=10**7, bytes_accessed=10**7, transcendentals=0),
    )(packed, target, now)
    n_z = n_member // 2
    share = n_obs // n_state
    dma = pltpu.SemaphoreType.DMA
    shared = pl.pallas_call(
        functools.partial(share_kernel, n_z, n_state),
        out_shape=jax.ShapeDtypeStruct((2, n_state, n_z, local_members, share), f32),
        in_specs=[VMEM],
        out_specs=VMEM,
        scratch_shapes=[
            pltpu.VMEM((n_state - 1, local_members, share), f32),
            dma((n_state - 1,)),
            dma((n_state - 1,)),
            dma((n_z - 1,)),
            dma((n_z - 1,)),
            dma((n_state - 1,)),
            dma((n_state - 1,)),
            dma((n_state,)),
            dma((n_state,)),
        ],
        compiler_params=pltpu.CompilerParams(
            collective_id=0, has_side_effects=True, vmem_limit_bytes=32 * 1024 * 1024
        ),
    )(part.reshape(local_members, n_state, share).transpose(1, 0, 2))
    y0 = shared.transpose(2, 0, 3, 1, 4).reshape(members, n_obs)
    ybt, dy, q = pl.pallas_call(
        observed_kernel,
        out_shape=[
            jax.ShapeDtypeStruct((n_obs, members), jnp.bfloat16),
            jax.ShapeDtypeStruct((members, n_obs), jnp.bfloat16),
            jax.ShapeDtypeStruct((n_obs, 8), f32),
        ],
        in_specs=[VMEM] * 3,
        out_specs=[VMEM] * 3,
        scratch_shapes=[pltpu.VMEM((members, n_obs), f32)],
        compiler_params=pltpu.CompilerParams(vmem_limit_bytes=40 * 1024 * 1024),
        cost_estimate=pl.CostEstimate(flops=10**9, bytes_accessed=10**7, transcendentals=0),
    )(y0, by_obs, by_field)
    backs = []
    for p in range(PARTS):
        result = pl.pallas_call(
            functools.partial(cells_kernel, cols // TILE, p * width),
            out_shape=jax.ShapeDtypeStruct(cells[p].shape, f32),
            in_specs=[SMEM, SMEM] + [VMEM] * 5,
            out_specs=VMEM,
            scratch_shapes=[
                pltpu.VMEM((tile_rows, BLK, LANES), f32),
                pltpu.VMEM((BLK, TILE), f32),
            ],
            compiler_params=pltpu.CompilerParams(vmem_limit_bytes=40 * 1024 * 1024),
            cost_estimate=pl.CostEstimate(
                flops=2 * 10**10, bytes_accessed=10**7, transcendentals=0
            ),
        )(jnp.reshape(first_row, (1,)).astype(jnp.int32), span, cells[p], by_obs, ybt, dy, q)
        backs.append(
            lax.all_to_all(result, "member", split_axis=1, concat_axis=0, tiled=True)
        )
    return jnp.concatenate([back.transpose(1, 0, 2) for back in backs], axis=2)


def solution(mesh):
    in_specs = (P("member", "state", None), P("state", None), P(), P(), P(), P(), P(), P())
    out_specs = P("member", "state", None)
    return jax.shard_map(
        on_device, mesh=mesh, in_specs=in_specs, out_specs=out_specs, check_vma=False
    )
```

```python
import functools

import jax
import jax.numpy as jnp
from jax import lax
from jax.experimental import pallas as pl
from jax.experimental.pallas import tpu as pltpu
from jax.sharding import PartitionSpec as P

BLK = 512
NBLK = 6
LANES = 128
TILE = 256
PARTS = 2
EPS = 1e-06
MESH = pl.DeviceIdType.MESH
VMEM = pl.BlockSpec(memory_space=pltpu.VMEM)
SMEM = pl.BlockSpec(memory_space=pltpu.SMEM)


def forecast(u, coef):
    peers = lax.axis_size("state")
    up = [(i, i + 1) for i in range(peers - 1)]
    down = [(j, i) for i, j in up]
    rows = u.shape[1]
    last = jnp.concatenate([u[:, rows - 2 :], coef[None, rows - 2 :]], axis=0)
    first = jnp.concatenate([u[:, :2], coef[None, :2]], axis=0)
    before = lax.ppermute(last, "state", up)
    after = lax.ppermute(first, "state", down)
    current = jnp.concatenate([before[:-1], u, after[:-1]], axis=1)
    field = jnp.concatenate([before[-1], coef, after[-1]], axis=0)
    for _ in range(2):
        center = current[:, 1:-1]
        field = field[1:-1]
        vertical = current[:, 2:] + current[:, :-2]
        sideways = jnp.pad(center[:, :, 1:], ((0, 0), (0, 0), (0, 1))) + jnp.pad(
            center[:, :, :-1], ((0, 0), (0, 0), (1, 0))
        )
        current = center + field * (vertical + sideways - 4.0 * center)
    return current


def pick_kernel(where_ref, lane_ref, field_ref, out_ref):
    members = field_ref.shape[1]
    lane = lax.broadcasted_iota(jnp.int32, (members, LANES), 1)

    def chunk(j, _):
        def step(t, acc):
            for i in range(16):
                k = j * LANES + t * 16 + i
                packed = where_ref[k]
                local = lax.shift_right_logical(packed, 15)
                start = pl.multiple_of(packed & 0x7F80, LANES)
                part = field_ref[local, :, pl.ds(start, LANES)]
                turned = pltpu.roll(part, packed & (LANES - 1), 1)
                acc = jnp.where(lane == lane_ref[k], turned, acc)
            return acc

        acc = lax.fori_loop(0, LANES // 16, step, jnp.zeros((members, LANES), jnp.float32))
        out_ref[:, pl.ds(pl.multiple_of(j * LANES, LANES), LANES)] = acc
        return 0

    lax.fori_loop(0, out_ref.shape[1] // LANES, chunk, 0)


def share_kernel(
    n_z, n_state, part_ref, out_ref, slots, send_1, recv_1, send_2, recv_2, send_3, recv_3, send_4, recv_4
):
    mi = lax.axis_index("member")
    si = lax.axis_index("state")
    core = lax.rem(mi, 2)
    z = lax.div(mi, 2)
    sibling = (z * 2 + 1 - core, si)
    across = [(mi, lax.rem(si + d, n_state)) for d in range(1, n_state)]
    along = [(lax.rem(z + d, n_z) * 2 + core, si) for d in range(1, n_z)]
    barrier = pltpu.get_barrier_semaphore()
    for peer in across + along + [sibling]:
        pl.semaphore_signal(barrier, inc=1, device_id=peer, device_id_type=MESH)
    pl.semaphore_wait(barrier, n_state + n_z - 1)

    def send(source, target, send_sem, recv_sem, peer):
        copy = pltpu.make_async_remote_copy(
            src_ref=source,
            dst_ref=target,
            send_sem=send_sem,
            recv_sem=recv_sem,
            device_id=peer,
            device_id_type=MESH,
        )
        copy.start()
        return copy

    first = [
        send(part_ref.at[peer[1]], slots.at[d], send_1.at[d], recv_1.at[d], peer)
        for d, peer in enumerate(across)
    ]
    total = part_ref[si]
    for d in range(n_state - 1):
        first[d].wait()
        total = total + slots[d]
    out_ref[core, si, z] = total
    mine = out_ref.at[core, si, z]
    second = [
        send(mine, mine, send_2.at[d], recv_2.at[d], peer) for d, peer in enumerate(along)
    ]
    for copy in second:
        copy.wait()
    line = out_ref.at[core, si]
    third = [
        send(line, line, send_3.at[d], recv_3.at[d], peer) for d, peer in enumerate(across)
    ]
    last = [send(line, line, send_4.at[0], recv_4.at[0], sibling)]
    for d in range(1, n_state):
        third[d - 1].wait()
        other = out_ref.at[core, lax.rem(si + n_state - d, n_state)]
        last.append(send(other, other, send_4.at[d], recv_4.at[d], sibling))
    for copy in last:
        copy.wait()


def anomalies(values):
    return (values - jnp.mean(values, axis=0, keepdims=True)).astype(jnp.bfloat16)


def observed_kernel(y0_ref, pcol_ref, prow_ref, ybt_ref, dy_ref, q_ref, y_ref):
    members = y0_ref.shape[0]
    y_ref[...] = y0_ref[...]

    def block(b, _):
        own = pl.ds(pl.multiple_of(b * BLK, BLK), BLK)
        values = y_ref[:, own]
        mean = jnp.mean(values, axis=0, keepdims=True)
        anomaly = values - mean
        spread = jnp.sum(anomaly * anomaly, axis=0, keepdims=True) / (members - 1) + EPS
        observed = prow_ref[3:4, own]
        variance = prow_ref[4:5, own]
        post = spread * variance / (spread + variance)
        center = post * (mean / spread + observed / variance)
        shrink = jnp.sqrt(variance / (variance + spread)) - 1.0
        dy_ref[:, own] = (center - mean + shrink * anomaly).astype(jnp.bfloat16)
        turned = anomaly.T
        ybt_ref[own, :] = turned.astype(jnp.bfloat16)
        spread_c = jnp.sum(turned * turned, axis=1, keepdims=True) / (members - 1) + EPS
        q = jnp.sqrt(1.0 / (spread_c * (members - 1)))
        reach = pcol_ref[own, 2:3]
        q_ref[own, 0:1] = q
        q_ref[own, 1:2] = q / (reach * reach)

        def later(t, _):
            at = pl.ds(pl.multiple_of(t * BLK, BLK), BLK)
            y = y_ref[:, at]
            cov = jnp.dot(ybt_ref[own, :], anomalies(y), preferred_element_type=jnp.float32)
            gap_r = prow_ref[0:1, at] - pcol_ref[own, 0:1]
            gap_c = prow_ref[1:2, at] - pcol_ref[own, 1:2]
            far = (gap_r * gap_r + gap_c * gap_c) * q_ref[own, 1:2]
            w = jnp.maximum(q_ref[own, 0:1] - far, 0.0)
            gain = (w * w * cov).astype(jnp.bfloat16)
            y_ref[:, at] = y + jnp.dot(dy_ref[:, own], gain, preferred_element_type=jnp.float32)
            return 0

        lax.fori_loop(b + 1, NBLK, later, 0)
        return 0

    lax.fori_loop(0, NBLK, block, 0)


def cells_kernel(
    n_tiles, first_col, base_ref, span_ref, x_ref, pcol_ref, ybt_ref, dy_ref, q_ref, out_ref, near_ref, across_ref
):
    rows, members, cols = out_ref.shape
    base = base_ref[0].astype(jnp.float32)
    out_ref[...] = x_ref[:, :, first_col : first_col + cols]
    groups = TILE // LANES
    together = next(n for n in (8, 4, 2, 1) if rows % n == 0)

    def block(b, _):
        own = pl.ds(pl.multiple_of(b * BLK, BLK), BLK)
        obs_r = pcol_ref[own, 0:1]
        q = q_ref[own, 0:1]
        inv = q_ref[own, 1:2]
        for r in range(rows):
            gap = base + float(r) - obs_r
            near_ref[r] = jnp.broadcast_to(q - gap * gap * inv, (BLK, LANES))

        def column(t, _):
            at = pl.ds(pl.multiple_of(t * TILE, TILE), TILE)
            place = lax.broadcasted_iota(jnp.int32, (1, TILE), 1) + (t * TILE + first_col)
            place = place.astype(jnp.float32)
            entry = (b * n_tiles + first_col // TILE + t) * 2
            lead = span_ref[entry] * LANES
            count = span_ref[entry + 1]

            def window(size):
                mine = pl.ds(pl.multiple_of(lead, LANES), size)
                ours = pl.ds(pl.multiple_of(b * BLK + lead, LANES), size)
                gap = place - pcol_ref[ours, 1:2]
                across_ref[0:size, :] = gap * gap * q_ref[ours, 1:2]

                def row(g, _):
                    xs = [out_ref[g * together + i, :, at] for i in range(together)]
                    x = jnp.concatenate(xs, axis=1)
                    cov = jnp.dot(ybt_ref[ours, :], anomalies(x), preferred_element_type=jnp.float32)
                    far = across_ref[0:size, :]
                    gains = []
                    for i in range(together):
                        near = jnp.concatenate([near_ref[g * together + i, mine, :]] * groups, axis=1)
                        w = jnp.maximum(near - far, 0.0)
                        gains.append(
                            (w * w * cov[:, i * TILE : (i + 1) * TILE]).astype(jnp.bfloat16)
                        )
                    x = x + jnp.dot(
                        dy_ref[:, ours],
                        jnp.concatenate(gains, axis=1),
                        preferred_element_type=jnp.float32,
                    )
                    for i in range(together):
                        out_ref[g * together + i, :, at] = x[:, i * TILE : (i + 1) * TILE]
                    return 0

                lax.fori_loop(0, rows // together, row, 0)

            for parts in range(1, BLK // LANES + 1):
                pl.when(count == parts)(functools.partial(window, parts * LANES))
            return 0

        lax.fori_loop(0, cols // TILE, column, 0)
        return 0

    lax.fori_loop(0, NBLK, block, 0)


def by_column(table, reach, cols):
    blocks = table.reshape(NBLK, BLK, table.shape[1])
    key = blocks[:, :, 1].astype(jnp.int32) * BLK + jnp.arange(BLK, dtype=jnp.int32)
    rank = jnp.sum((key[:, None, :] < key[:, :, None]).astype(jnp.int32), axis=2)
    chosen = (jnp.arange(BLK, dtype=jnp.int32)[None, :, None] == rank[:, None, :]).astype(jnp.float32)
    ordered = jnp.einsum("bpi,bif->bpf", chosen, blocks, precision=lax.Precision.HIGHEST)
    column = blocks[:, None, :, 1].astype(jnp.int32)
    start = (jnp.arange(cols // TILE, dtype=jnp.int32) * TILE)[None, :, None]
    before = jnp.sum((column < start - reach).astype(jnp.int32), axis=2)
    until = jnp.sum((column < start + TILE + reach).astype(jnp.int32), axis=2)
    lead = jnp.minimum(before // LANES, BLK // LANES - 1)
    count = jnp.maximum((until + LANES - 1) // LANES - lead, 0)
    return ordered.reshape(table.shape), jnp.stack([lead, count], axis=-1).reshape(-1)


def on_device(prior, coef, observations, obs_variance, obs_row, obs_col, obs_radius, block_order):
    n_member = lax.axis_size("member")
    n_state = lax.axis_size("state")
    local_members, local_rows, cols = prior.shape
    members = local_members * n_member
    n_obs = block_order.shape[0]
    f32 = jnp.float32
    table = jnp.stack(
        [
            obs_row.astype(f32),
            obs_col.astype(f32),
            obs_radius.astype(f32),
            observations,
            obs_variance,
        ]
        + [jnp.zeros((n_obs,), f32)] * 3,
        axis=1,
    )
    by_obs, span = by_column(jnp.take(table, block_order, axis=0), jnp.max(obs_radius), cols)
    by_field = by_obs.T
    row_i = by_field[0].astype(jnp.int32)
    col_i = by_field[1].astype(jnp.int32)

    now = forecast(prior, coef).transpose(1, 0, 2)
    base_row = lax.axis_index("state") * local_rows
    tile_rows = local_rows // n_member
    first_row = base_row + lax.axis_index("member") * tile_rows
    width = cols // PARTS
    cells = lax.all_to_all(now, "member", split_axis=0, concat_axis=1, tiled=True)

    local = row_i - base_row
    inside = (local >= 0) & (local < local_rows)
    index = jnp.arange(n_obs, dtype=jnp.int32)
    turn = (index - col_i) & (LANES - 1)
    packed = (jnp.where(inside, local, 0) << 15) | (col_i & 0x7F80) | turn
    target = jnp.where(inside, index & (LANES - 1), -1)
    part = pl.pallas_call(
        pick_kernel,
        out_shape=jax.ShapeDtypeStruct((local_members, n_obs), f32),
        in_specs=[SMEM, SMEM, VMEM],
        out_specs=VMEM,
        compiler_params=pltpu.CompilerParams(vmem_limit_bytes=32 * 1024 * 1024),
        cost_estimate=pl.CostEstimate(flops=10**7, bytes_accessed=10**7, transcendentals=0),
    )(packed, target, now)
    n_z = n_member // 2
    share = n_obs // n_state
    dma = pltpu.SemaphoreType.DMA
    shared = pl.pallas_call(
        functools.partial(share_kernel, n_z, n_state),
        out_shape=jax.ShapeDtypeStruct((2, n_state, n_z, local_members, share), f32),
        in_specs=[VMEM],
        out_specs=VMEM,
        scratch_shapes=[
            pltpu.VMEM((n_state - 1, local_members, share), f32),
            dma((n_state - 1,)),
            dma((n_state - 1,)),
            dma((n_z - 1,)),
            dma((n_z - 1,)),
            dma((n_state - 1,)),
            dma((n_state - 1,)),
            dma((n_state,)),
            dma((n_state,)),
        ],
        compiler_params=pltpu.CompilerParams(
            collective_id=0, has_side_effects=True, vmem_limit_bytes=32 * 1024 * 1024
        ),
    )(part.reshape(local_members, n_state, share).transpose(1, 0, 2))
    y0 = shared.transpose(2, 0, 3, 1, 4).reshape(members, n_obs)
    ybt, dy, q = pl.pallas_call(
        observed_kernel,
        out_shape=[
            jax.ShapeDtypeStruct((n_obs, members), jnp.bfloat16),
            jax.ShapeDtypeStruct((members, n_obs), jnp.bfloat16),
            jax.ShapeDtypeStruct((n_obs, 8), f32),
        ],
        in_specs=[VMEM] * 3,
        out_specs=[VMEM] * 3,
        scratch_shapes=[pltpu.VMEM((members, n_obs), f32)],
        compiler_params=pltpu.CompilerParams(vmem_limit_bytes=40 * 1024 * 1024),
        cost_estimate=pl.CostEstimate(flops=10**9, bytes_accessed=10**7, transcendentals=0),
    )(y0, by_obs, by_field)
    backs = []
    for p in range(PARTS):
        result = pl.pallas_call(
            functools.partial(cells_kernel, cols // TILE, p * width),
            out_shape=jax.ShapeDtypeStruct((tile_rows, members, width), f32),
            in_specs=[SMEM, SMEM] + [VMEM] * 5,
            out_specs=VMEM,
            scratch_shapes=[
                pltpu.VMEM((tile_rows, BLK, LANES), f32),
                pltpu.VMEM((BLK, TILE), f32),
            ],
            compiler_params=pltpu.CompilerParams(vmem_limit_bytes=40 * 1024 * 1024),
            cost_estimate=pl.CostEstimate(
                flops=2 * 10**10, bytes_accessed=10**7, transcendentals=0
            ),
        )(jnp.reshape(first_row, (1,)).astype(jnp.int32), span, cells, by_obs, ybt, dy, q)
        backs.append(
            lax.all_to_all(result, "member", split_axis=1, concat_axis=0, tiled=True)
        )
    return jnp.concatenate([back.transpose(1, 0, 2) for back in backs], axis=2)


def solution(mesh):
    in_specs = (P("member", "state", None), P("state", None), P(), P(), P(), P(), P(), P())
    out_specs = P("member", "state", None)
    return jax.shard_map(
        on_device, mesh=mesh, in_specs=in_specs, out_specs=out_specs, check_vma=False
    )
```

```python
import functools

import jax
import jax.numpy as jnp
from jax import lax
from jax.experimental import pallas as pl
from jax.experimental.pallas import tpu as pltpu
from jax.sharding import PartitionSpec as P

BLK = 512
NBLK = 6
LANES = 128
TILE = 256
PARTS = 2
EPS = 1e-06
MESH = pl.DeviceIdType.MESH
VMEM = pl.BlockSpec(memory_space=pltpu.VMEM)
SMEM = pl.BlockSpec(memory_space=pltpu.SMEM)


def forecast(u, coef):
    peers = lax.axis_size("state")
    up = [(i, i + 1) for i in range(peers - 1)]
    down = [(j, i) for i, j in up]
    rows = u.shape[1]
    last = jnp.concatenate([u[:, rows - 2 :], coef[None, rows - 2 :]], axis=0)
    first = jnp.concatenate([u[:, :2], coef[None, :2]], axis=0)
    before = lax.ppermute(last, "state", up)
    after = lax.ppermute(first, "state", down)
    current = jnp.concatenate([before[:-1], u, after[:-1]], axis=1)
    field = jnp.concatenate([before[-1], coef, after[-1]], axis=0)
    for _ in range(2):
        center = current[:, 1:-1]
        field = field[1:-1]
        vertical = current[:, 2:] + current[:, :-2]
        sideways = jnp.pad(center[:, :, 1:], ((0, 0), (0, 0), (0, 1))) + jnp.pad(
            center[:, :, :-1], ((0, 0), (0, 0), (1, 0))
        )
        current = center + field * (vertical + sideways - 4.0 * center)
    return current


def pick_kernel(where_ref, inside_ref, field_ref, out_ref):
    members = field_ref.shape[1]
    lane = lax.broadcasted_iota(jnp.int32, (members, LANES), 1)

    def chunk(j, _):
        acc = jnp.zeros((members, LANES), jnp.float32)
        for i in range(LANES):
            packed = where_ref[j * LANES + i]
            local = lax.shift_right_logical(packed, 15)
            start = pl.multiple_of(packed & 0x7F80, LANES)
            part = field_ref[local, :, pl.ds(start, LANES)]
            turned = pltpu.roll(part, packed & (LANES - 1), 1)
            acc = jnp.where(lane == i, turned, acc)
        at = pl.ds(pl.multiple_of(j * LANES, LANES), LANES)
        out_ref[:, at] = jnp.where(inside_ref[:, at] > 0, acc, 0.0)
        return 0

    lax.fori_loop(0, out_ref.shape[1] // LANES, chunk, 0)


def share_kernel(
    n_z, n_state, part_ref, out_ref, slots, send_1, recv_1, send_2, recv_2, send_3, recv_3, send_4, recv_4
):
    mi = lax.axis_index("member")
    si = lax.axis_index("state")
    core = lax.rem(mi, 2)
    z = lax.div(mi, 2)
    sibling = (z * 2 + 1 - core, si)
    across = [(mi, lax.rem(si + d, n_state)) for d in range(1, n_state)]
    along = [(lax.rem(z + d, n_z) * 2 + core, si) for d in range(1, n_z)]
    barrier = pltpu.get_barrier_semaphore()
    for peer in across + along + [sibling]:
        pl.semaphore_signal(barrier, inc=1, device_id=peer, device_id_type=MESH)
    pl.semaphore_wait(barrier, n_state + n_z - 1)

    def send(source, target, send_sem, recv_sem, peer):
        copy = pltpu.make_async_remote_copy(
            src_ref=source,
            dst_ref=target,
            send_sem=send_sem,
            recv_sem=recv_sem,
            device_id=peer,
            device_id_type=MESH,
        )
        copy.start()
        return copy

    first = [
        send(part_ref.at[peer[1]], slots.at[d], send_1.at[d], recv_1.at[d], peer)
        for d, peer in enumerate(across)
    ]
    total = part_ref[si]
    for d in range(n_state - 1):
        first[d].wait()
        total = total + slots[d]
    out_ref[core, si, z] = total
    mine = out_ref.at[core, si, z]
    second = [
        send(mine, mine, send_2.at[d], recv_2.at[d], peer) for d, peer in enumerate(along)
    ]
    for copy in second:
        copy.wait()
    line = out_ref.at[core, si]
    third = [
        send(line, line, send_3.at[d], recv_3.at[d], peer) for d, peer in enumerate(across)
    ]
    last = [send(line, line, send_4.at[0], recv_4.at[0], sibling)]
    for d in range(1, n_state):
        third[d - 1].wait()
        other = out_ref.at[core, lax.rem(si + n_state - d, n_state)]
        last.append(send(other, other, send_4.at[d], recv_4.at[d], sibling))
    for copy in last:
        copy.wait()


def anomalies(values):
    return (values - jnp.mean(values, axis=0, keepdims=True)).astype(jnp.bfloat16)


def observed_kernel(y0_ref, pcol_ref, prow_ref, ybt_ref, dy_ref, q_ref, y_ref):
    members = y0_ref.shape[0]
    y_ref[...] = y0_ref[...]

    def block(b, _):
        own = pl.ds(pl.multiple_of(b * BLK, BLK), BLK)
        values = y_ref[:, own]
        mean = jnp.mean(values, axis=0, keepdims=True)
        anomaly = values - mean
        spread = jnp.sum(anomaly * anomaly, axis=0, keepdims=True) / (members - 1) + EPS
        observed = prow_ref[3:4, own]
        variance = prow_ref[4:5, own]
        post = spread * variance / (spread + variance)
        center = post * (mean / spread + observed / variance)
        shrink = jnp.sqrt(variance / (variance + spread)) - 1.0
        dy_ref[:, own] = (center - mean + shrink * anomaly).astype(jnp.bfloat16)
        turned = anomaly.T
        ybt_ref[own, :] = turned.astype(jnp.bfloat16)
        spread_c = jnp.sum(turned * turned, axis=1, keepdims=True) / (members - 1) + EPS
        q = jnp.sqrt(1.0 / (spread_c * (members - 1)))
        reach = pcol_ref[own, 2:3]
        q_ref[own, 0:1] = q
        q_ref[own, 1:2] = q / (reach * reach)

        def later(t, _):
            at = pl.ds(pl.multiple_of(t * BLK, BLK), BLK)
            y = y_ref[:, at]
            cov = jnp.dot(ybt_ref[own, :], anomalies(y), preferred_element_type=jnp.float32)
            gap_r = prow_ref[0:1, at] - pcol_ref[own, 0:1]
            gap_c = prow_ref[1:2, at] - pcol_ref[own, 1:2]
            far = (gap_r * gap_r + gap_c * gap_c) * q_ref[own, 1:2]
            w = jnp.maximum(q_ref[own, 0:1] - far, 0.0)
            gain = (w * w * cov).astype(jnp.bfloat16)
            y_ref[:, at] = y + jnp.dot(dy_ref[:, own], gain, preferred_element_type=jnp.float32)
            return 0

        lax.fori_loop(b + 1, NBLK, later, 0)
        return 0

    lax.fori_loop(0, NBLK, block, 0)


def cells_kernel(
    n_tiles, first_col, base_ref, span_ref, x_ref, pcol_ref, ybt_ref, dy_ref, q_ref, out_ref, near_ref, across_ref
):
    rows, members, cols = out_ref.shape
    base = base_ref[0].astype(jnp.float32)
    out_ref[...] = x_ref[:, :, first_col : first_col + cols]
    groups = TILE // LANES
    together = next(n for n in (8, 4, 2, 1) if rows % n == 0)

    def block(b, _):
        own = pl.ds(pl.multiple_of(b * BLK, BLK), BLK)
        obs_r = pcol_ref[own, 0:1]
        q = q_ref[own, 0:1]
        inv = q_ref[own, 1:2]
        for r in range(rows):
            gap = base + float(r) - obs_r
            near_ref[r] = jnp.broadcast_to(q - gap * gap * inv, (BLK, LANES))

        def column(t, _):
            at = pl.ds(pl.multiple_of(t * TILE, TILE), TILE)
            place = lax.broadcasted_iota(jnp.int32, (1, TILE), 1) + (t * TILE + first_col)
            place = place.astype(jnp.float32)
            entry = (b * n_tiles + first_col // TILE + t) * 2
            lead = span_ref[entry] * LANES
            count = span_ref[entry + 1]

            def window(size):
                mine = pl.ds(pl.multiple_of(lead, LANES), size)
                ours = pl.ds(pl.multiple_of(b * BLK + lead, LANES), size)
                gap = place - pcol_ref[ours, 1:2]
                across_ref[0:size, :] = gap * gap * q_ref[ours, 1:2]

                def row(g, _):
                    xs = [out_ref[g * together + i, :, at] for i in range(together)]
                    x = jnp.concatenate(xs, axis=1)
                    cov = jnp.dot(ybt_ref[ours, :], anomalies(x), preferred_element_type=jnp.float32)
                    far = across_ref[0:size, :]
                    gains = []
                    for i in range(together):
                        near = jnp.concatenate([near_ref[g * together + i, mine, :]] * groups, axis=1)
                        w = jnp.maximum(near - far, 0.0)
                        gains.append(
                            (w * w * cov[:, i * TILE : (i + 1) * TILE]).astype(jnp.bfloat16)
                        )
                    x = x + jnp.dot(
                        dy_ref[:, ours],
                        jnp.concatenate(gains, axis=1),
                        preferred_element_type=jnp.float32,
                    )
                    for i in range(together):
                        out_ref[g * together + i, :, at] = x[:, i * TILE : (i + 1) * TILE]
                    return 0

                lax.fori_loop(0, rows // together, row, 0)

            for parts in range(1, BLK // LANES + 1):
                pl.when(count == parts)(functools.partial(window, parts * LANES))
            return 0

        lax.fori_loop(0, cols // TILE, column, 0)
        return 0

    lax.fori_loop(0, NBLK, block, 0)


def by_column(table, reach, cols):
    blocks = table.reshape(NBLK, BLK, table.shape[1])
    key = blocks[:, :, 1].astype(jnp.int32) * BLK + jnp.arange(BLK, dtype=jnp.int32)
    rank = jnp.sum((key[:, None, :] < key[:, :, None]).astype(jnp.int32), axis=2)
    chosen = (jnp.arange(BLK, dtype=jnp.int32)[None, :, None] == rank[:, None, :]).astype(jnp.float32)
    ordered = jnp.einsum("bpi,bif->bpf", chosen, blocks, precision=lax.Precision.HIGHEST)
    column = blocks[:, None, :, 1].astype(jnp.int32)
    start = (jnp.arange(cols // TILE, dtype=jnp.int32) * TILE)[None, :, None]
    before = jnp.sum((column < start - reach).astype(jnp.int32), axis=2)
    until = jnp.sum((column < start + TILE + reach).astype(jnp.int32), axis=2)
    lead = jnp.minimum(before // LANES, BLK // LANES - 1)
    count = jnp.maximum((until + LANES - 1) // LANES - lead, 0)
    return ordered.reshape(table.shape), jnp.stack([lead, count], axis=-1).reshape(-1)


def on_device(prior, coef, observations, obs_variance, obs_row, obs_col, obs_radius, block_order):
    n_member = lax.axis_size("member")
    n_state = lax.axis_size("state")
    local_members, local_rows, cols = prior.shape
    members = local_members * n_member
    n_obs = block_order.shape[0]
    f32 = jnp.float32
    table = jnp.stack(
        [
            obs_row.astype(f32),
            obs_col.astype(f32),
            obs_radius.astype(f32),
            observations,
            obs_variance,
        ]
        + [jnp.zeros((n_obs,), f32)] * 3,
        axis=1,
    )
    by_obs, span = by_column(jnp.take(table, block_order, axis=0), jnp.max(obs_radius), cols)
    by_field = by_obs.T
    row_i = by_field[0].astype(jnp.int32)
    col_i = by_field[1].astype(jnp.int32)

    now = forecast(prior, coef).transpose(1, 0, 2)
    base_row = lax.axis_index("state") * local_rows
    tile_rows = local_rows // n_member
    first_row = base_row + lax.axis_index("member") * tile_rows
    width = cols // PARTS
    cells = lax.all_to_all(now, "member", split_axis=0, concat_axis=1, tiled=True)

    local = row_i - base_row
    inside = (local >= 0) & (local < local_rows)
    index = jnp.arange(n_obs, dtype=jnp.int32)
    turn = (index - col_i) & (LANES - 1)
    packed = (jnp.where(inside, local, 0) << 15) | (col_i & 0x7F80) | turn
    target = inside.astype(jnp.int32)[None, :]
    part = pl.pallas_call(
        pick_kernel,
        out_shape=jax.ShapeDtypeStruct((local_members, n_obs), f32),
        in_specs=[SMEM, VMEM, VMEM],
        out_specs=VMEM,
        compiler_params=pltpu.CompilerParams(vmem_limit_bytes=32 * 1024 * 1024),
        cost_estimate=pl.CostEstimate(flops=10**7, bytes_accessed=10**7, transcendentals=0),
    )(packed, target, now)
    n_z = n_member // 2
    share = n_obs // n_state
    dma = pltpu.SemaphoreType.DMA
    shared = pl.pallas_call(
        functools.partial(share_kernel, n_z, n_state),
        out_shape=jax.ShapeDtypeStruct((2, n_state, n_z, local_members, share), f32),
        in_specs=[VMEM],
        out_specs=VMEM,
        scratch_shapes=[
            pltpu.VMEM((n_state - 1, local_members, share), f32),
            dma((n_state - 1,)),
            dma((n_state - 1,)),
            dma((n_z - 1,)),
            dma((n_z - 1,)),
            dma((n_state - 1,)),
            dma((n_state - 1,)),
            dma((n_state,)),
            dma((n_state,)),
        ],
        compiler_params=pltpu.CompilerParams(
            collective_id=0, has_side_effects=True, vmem_limit_bytes=32 * 1024 * 1024
        ),
    )(part.reshape(local_members, n_state, share).transpose(1, 0, 2))
    y0 = shared.transpose(2, 0, 3, 1, 4).reshape(members, n_obs)
    ybt, dy, q = pl.pallas_call(
        observed_kernel,
        out_shape=[
            jax.ShapeDtypeStruct((n_obs, members), jnp.bfloat16),
            jax.ShapeDtypeStruct((members, n_obs), jnp.bfloat16),
            jax.ShapeDtypeStruct((n_obs, 8), f32),
        ],
        in_specs=[VMEM] * 3,
        out_specs=[VMEM] * 3,
        scratch_shapes=[pltpu.VMEM((members, n_obs), f32)],
        compiler_params=pltpu.CompilerParams(vmem_limit_bytes=40 * 1024 * 1024),
        cost_estimate=pl.CostEstimate(flops=10**9, bytes_accessed=10**7, transcendentals=0),
    )(y0, by_obs, by_field)
    backs = []
    for p in range(PARTS):
        result = pl.pallas_call(
            functools.partial(cells_kernel, cols // TILE, p * width),
            out_shape=jax.ShapeDtypeStruct((tile_rows, members, width), f32),
            in_specs=[SMEM, SMEM] + [VMEM] * 5,
            out_specs=VMEM,
            scratch_shapes=[
                pltpu.VMEM((tile_rows, BLK, LANES), f32),
                pltpu.VMEM((BLK, TILE), f32),
            ],
            compiler_params=pltpu.CompilerParams(vmem_limit_bytes=40 * 1024 * 1024),
            cost_estimate=pl.CostEstimate(
                flops=2 * 10**10, bytes_accessed=10**7, transcendentals=0
            ),
        )(jnp.reshape(first_row, (1,)).astype(jnp.int32), span, cells, by_obs, ybt, dy, q)
        backs.append(
            lax.all_to_all(result, "member", split_axis=1, concat_axis=0, tiled=True)
        )
    return jnp.concatenate([back.transpose(1, 0, 2) for back in backs], axis=2)


def solution(mesh):
    in_specs = (P("member", "state", None), P("state", None), P(), P(), P(), P(), P(), P())
    out_specs = P("member", "state", None)
    return jax.shard_map(
        on_device, mesh=mesh, in_specs=in_specs, out_specs=out_specs, check_vma=False
    )
```
